512 devices in a mesh: dp: 16 (over y, x), col: 32 (over z, core).
Axes of the slice: x: 4, y: 4, z: 16, core: 2. Of those that a mesh axis runs over, the one named last changes fastest.
Arguments:
- grad_parts: bfloat16 [16, 2048, 7168], P('dp', None, 'col'), may hold values from -1.5 to 1.5
- left_basis: bfloat16 [2048, 2048], P('dp'), may hold values from -0.125 to 0.125
- right_basis: bfloat16 [7168, 7168], P('col', 'dp'), may hold values from -0.0625 to 0.0625
- first_moment: float32 [7168, 2048], P('dp', 'col'), may hold values from -0.6 to 0.6
- second_moment: float32 [7168, 2048], P('dp', 'col'), may hold values from 0.005 to 0.5
Outputs:
- left_gram: float32 [2048, 2048], P('dp', 'col')
- new_first: float32 [7168, 2048], P('dp', 'col')
- new_second: float32 [7168, 2048], P('dp', 'col')
- direction: float32 [2048, 7168], P('dp', 'col')
The draws below stay inside these ranges and needn't reach their ends.
All inputs are finite; a program needn't handle non-finite values.
Results may differ from the reference program's by a relative error of at most 0.035.
Values may be sent and summed in bfloat16 or wider, within the bound.
No kernel may reach another device: no remote copies, remote signals or barrier semaphores. Data moves between devices by JAX's collectives and lax.ppermute only.
A program may use at most 64 MiB of HBM per device.

```python
import math
import jax
import jax.numpy as jnp
from jax import lax

FF = 2048
D = 7168
REPLICAS = 16
N_DP = 16
N_COL = 32


def level_of(rng, dims, shards, smallest, largest):
    factor_of = 1.0
    for axis_at, parts in shards:
        draws = jax.random.uniform(jax.random.fold_in(jax.random.fold_in(rng, 6), axis_at), (parts,), jnp.float32, smallest / len(shards), largest / len(shards))
        factor_of = factor_of * jnp.repeat(jnp.exp(draws), dims[axis_at] // parts).reshape((-1,) + (1,) * (len(dims) - 1 - axis_at))
    return factor_of


def gaussian(key, shape, deviation, limit, cuts=(), kind=jnp.bfloat16):
    array = jax.random.normal(key, shape, jnp.float32) * deviation
    if len(cuts) > 0:
        array = level_of(key, shape, cuts, -0.22, 0.18) * array
    return jnp.clip(array, min=-limit, max=limit).astype(kind)


def setup_inputs(seed: int = 0) -> dict:
    keys = jax.random.split(jax.random.key(seed), 6)
    return {
        "grad_parts": gaussian(keys[0], (REPLICAS, FF, D), 0.25, 1.5, ((0, 16), (2, 32))),
        "left_basis": gaussian(keys[1], (FF, FF), FF ** -0.5, 0.125, ((0, 16),)),
        "right_basis": gaussian(keys[2], (D, D), D ** -0.5, 0.0625, ((0, 32), (1, 16))),
        "first_moment": gaussian(keys[3], (D, FF), 0.1, 0.6, ((0, 16), (1, 32)), jnp.float32),
        "second_moment": jnp.clip(jnp.exp(math.log(0.5) - 4.6051702 * jax.random.uniform(keys[4], (D, FF), jnp.float32) ** level_of(keys[4], (D, FF), ((0, 16), (1, 32)), -0.2, 0.2)), 0.005, 0.5),
    }


def rounded_add(running, term):
    return running + lax.optimization_barrier(term.astype(jnp.bfloat16)).astype(jnp.float32)

def reference(grad_parts, left_basis, right_basis, first_moment, second_moment):
    col_block = D // N_COL
    row_block = FF // N_DP
    turn_block = D // N_DP
    grad = lax.optimization_barrier(jnp.sum(grad_parts.astype(jnp.float32), axis=0)).astype(jnp.bfloat16)
    grad_cols = grad.reshape(FF, N_COL, col_block).transpose(1, 0, 2)

    def gram_step(running, block):
        term = jnp.dot(block, block.T, preferred_element_type=jnp.float32) / D
        return (rounded_add(running, term), None)
    left_gram, unused = lax.scan(gram_step, jnp.zeros((FF, FF), jnp.float32), grad_cols)
    left_rows = left_basis.reshape(N_DP, row_block, FF)
    grad_rows = grad.reshape(N_DP, row_block, D)

    def left_step(running, pair):
        basis_rows, data_rows = pair
        term = lax.dot_general(basis_rows, data_rows, (((0,), (0,)), ((), ())), preferred_element_type=jnp.float32)
        return (rounded_add(running, term), None)
    summed, unused = lax.scan(left_step, jnp.zeros((FF, D), jnp.float32), (left_rows, grad_rows))
    turned = summed.astype(jnp.bfloat16)
    basis_blocks = right_basis.reshape(N_COL, col_block, D)
    turned_cols = turned.reshape(FF, N_COL, col_block).transpose(1, 0, 2)

    def right_step(running, pair):
        basis_rows, data_cols = pair
        term = lax.dot_general(basis_rows, data_cols, (((0,), (1,)), ((), ())), preferred_element_type=jnp.float32)
        return (rounded_add(running, term), None)
    rotated, unused = lax.scan(right_step, jnp.zeros((D, FF), jnp.float32), (basis_blocks, turned_cols))
    new_first = 0.9 * first_moment + 0.1 * rotated
    new_second = 0.95 * second_moment + 0.05 * rotated * rotated
    update = (new_first / 0.19 / (jnp.sqrt(new_second / 0.0975) + 1e-08)).astype(jnp.bfloat16)
    update_blocks = update.reshape(N_DP, turn_block, FF)
    basis_cols = right_basis.reshape(D, N_DP, turn_block).transpose(1, 0, 2)

    def back_step(running, pair):
        update_rows, basis_part = pair
        term = lax.dot_general(update_rows, basis_part, (((0,), (1,)), ((), ())), preferred_element_type=jnp.float32)
        return (rounded_add(running, term), None)
    summed_back, unused = lax.scan(back_step, jnp.zeros((FF, D), jnp.float32), (update_blocks, basis_cols))
    turned_back = summed_back.astype(jnp.bfloat16)
    direction = jnp.dot(left_basis, turned_back, preferred_element_type=jnp.float32)
    return (left_gram, new_first, new_second, direction)
```

```python
import jax
import jax.numpy as jnp
from jax import lax
from jax.sharding import Mesh, PartitionSpec as P

D = 7168
DP = ("y", "x")
F32 = jnp.float32
BF16 = jnp.bfloat16


def exchange(chunks, axes):
    return lax.all_to_all(chunks, axes, 0, 0, tiled=True)


def on_device(grad_parts, left_basis, right_basis, first_moment, second_moment):
    rows = left_basis.shape[0]
    cols = right_basis.shape[0]
    turns = right_basis.shape[1]
    n_dp = left_basis.shape[1] // rows
    n_z = lax.axis_size("z")
    sub = rows // n_dp
    half = rows // 2
    core = lax.axis_index("core")

    basis_z = lax.all_gather(right_basis, "z", axis=0, tiled=False)

    parts = grad_parts[0].T.reshape(cols, n_dp, rows).transpose(1, 0, 2)
    grad_t = jnp.sum(exchange(parts, DP).astype(F32), axis=0).astype(BF16)

    basis_p = (
        left_basis.reshape(rows, n_z, n_dp, sub).transpose(0, 2, 1, 3).reshape(rows, n_dp, rows)
    )
    left_term = lax.dot_general(
        basis_p, grad_t, (((0,), (1,)), ((), ())), preferred_element_type=F32
    )
    turned = jnp.sum(exchange(left_term.astype(BF16), DP).astype(F32), axis=0).astype(BF16)
    turned = exchange(turned.reshape(n_z, sub, cols), "z")
    turned = exchange(jnp.broadcast_to(turned[None], (n_dp, n_z, sub, cols)), DP)

    grad_all = exchange(jnp.broadcast_to(grad_t[None], (n_dp, cols, rows)), DP)
    gram = lax.dot_general(
        grad_all, grad_t, (((1,), (0,)), ((), ())), preferred_element_type=F32
    ).reshape(n_z, 2, half, rows) / D
    mine = lax.dynamic_index_in_dim(gram, core, 1, keepdims=False)
    other = lax.dynamic_index_in_dim(gram, 1 - core, 1, keepdims=False)
    swap = [(0, 1), (1, 0)]
    mine = mine + lax.ppermute(other.astype(BF16), "core", swap).astype(F32)
    left_gram = lax.psum_scatter(mine, "z", scatter_dimension=0, tiled=False).T

    rotated = jnp.einsum("iztc,zcn->itn", turned, basis_z, preferred_element_type=F32)
    rotated = rotated.reshape(2, half, turns)
    mine = lax.dynamic_index_in_dim(rotated, core, 0, keepdims=False)
    other = lax.dynamic_index_in_dim(rotated, 1 - core, 0, keepdims=False)
    mine = mine + lax.ppermute(other.astype(BF16), "core", swap).astype(F32)
    new_first = 0.9 * first_moment.T + 0.1 * mine
    new_second = 0.95 * second_moment.T + 0.05 * mine * mine
    update = (new_first / 0.19 / (jnp.sqrt(new_second / 0.0975) + 1e-08)).astype(BF16)
    theirs = lax.ppermute(update, "core", swap)
    update = jnp.where(core == 0, jnp.stack([update, theirs]), jnp.stack([theirs, update]))
    update = update.reshape(rows, turns)

    back = jnp.einsum("mn,zcn->zmc", update, basis_z, preferred_element_type=F32).astype(BF16)
    back = back.reshape(n_z, n_dp, sub, cols).transpose(1, 0, 2, 3)
    back = jnp.sum(exchange(back, DP).astype(F32), axis=0).astype(BF16)
    back = exchange(back, "z")
    back = exchange(jnp.broadcast_to(back[None], (n_dp, n_z, sub, cols)), DP)
    direction = jnp.dot(
        basis_p.reshape(rows, n_dp * rows),
        back.reshape(n_dp * rows, cols),
        preferred_element_type=F32,
    )
    return (left_gram, new_first.T, new_second.T, direction)


def solution(mesh):
    n_dp, n_col = mesh.shape["dp"], mesh.shape["col"]
    side = int(round(n_dp**0.5))
    fine = Mesh(
        mesh.devices.reshape(side, side, n_col // 2, 2), ("y", "x", "z", "core")
    )
    dp, col = ("y", "x"), ("z", "core")
    in_specs = (P(dp, None, col), P(dp, None), P(col, dp), P(dp, col), P(dp, col))
    out_specs = (P(dp, col), P(dp, col), P(dp, col), P(dp, col))
    return jax.shard_map(
        on_device, mesh=fine, in_specs=in_specs, out_specs=out_specs, check_vma=False
    )
```

```python
import jax
import jax.numpy as jnp
from jax import lax
from jax.sharding import Mesh, PartitionSpec as P

D = 7168
DP = ("y", "x")
F32 = jnp.float32
BF16 = jnp.bfloat16
LANES = 128


def exchange(chunks, axes):
    return lax.all_to_all(chunks, axes, 0, 0, tiled=True)


def swap_cores(block):
    return lax.ppermute(block, "core", [(0, 1), (1, 0)])


def to_tiles(block):
    z, sub, cols = block.shape
    block = jnp.pad(block, ((0, 0), (0, 0), (0, 2 * LANES - cols)))
    return block.reshape(z, sub, 2, LANES).transpose(0, 2, 1, 3).reshape(z, 2 * sub, LANES)


def from_tiles(block, cols):
    z, rows, _ = block.shape
    block = block.reshape(z, 2, rows // 2, LANES).transpose(0, 2, 1, 3)
    return block.reshape(z, rows // 2, 2 * LANES)[:, :, :cols]


def on_device(grad_parts, left_basis, right_basis, first_moment, second_moment):
    rows = left_basis.shape[0]
    cols = right_basis.shape[0]
    turns = right_basis.shape[1]
    n_dp = left_basis.shape[1] // rows
    n_z = lax.axis_size("z")
    sub = rows // n_dp
    half = rows // 2
    core = lax.axis_index("core")

    def both(block):
        theirs = swap_cores(block)
        return jnp.where(core == 0, jnp.stack([block, theirs]), jnp.stack([theirs, block]))

    basis_z = lax.all_gather(right_basis, "z", axis=0, tiled=False)

    parts = grad_parts[0].T.reshape(cols, n_dp, rows).transpose(1, 0, 2)
    grad_t = jnp.sum(exchange(parts, DP).astype(F32), axis=0).astype(BF16)

    basis_p = (
        left_basis.reshape(rows, n_z, n_dp, sub).transpose(0, 2, 1, 3).reshape(rows, n_dp, rows)
    )
    left_term = lax.dot_general(
        basis_p, grad_t, (((0,), (1,)), ((), ())), preferred_element_type=F32
    )
    turned = exchange(left_term.astype(BF16), DP)
    turned, copies = lax.optimization_barrier(
        (turned, jnp.broadcast_to(grad_t[None], (n_dp, cols, rows)))
    )
    turned = jnp.sum(turned.astype(F32), axis=0).astype(BF16)
    turned, grad_all, moments = lax.optimization_barrier(
        (turned, exchange(copies, DP), both(jnp.stack([first_moment.T, second_moment.T])))
    )
    turned = exchange(turned.reshape(n_z, sub, cols), "z")

    gram = lax.dot_general(
        grad_all, grad_t, (((1,), (0,)), ((), ())), preferred_element_type=F32
    ).reshape(n_z, 2, half, rows) / D
    mine = lax.dynamic_index_in_dim(gram, core, 1, keepdims=False)
    other = lax.dynamic_index_in_dim(gram, 1 - core, 1, keepdims=False)
    gram = (mine + swap_cores(other.astype(BF16)).astype(F32)).astype(BF16)

    turned, gram = lax.optimization_barrier((turned, gram))
    turned = exchange(jnp.broadcast_to(turned[None], (n_dp, n_z, sub, cols)), DP)

    rotated = jnp.einsum("iztc,zcn->itn", turned, basis_z, preferred_element_type=F32)
    rotated = rotated.reshape(rows, turns)
    rotated = rotated + swap_cores(rotated.astype(BF16)).astype(F32)
    new_first = 0.9 * moments[:, 0].reshape(rows, turns) + 0.1 * rotated
    new_second = 0.95 * moments[:, 1].reshape(rows, turns) + 0.05 * rotated * rotated
    update = (new_first / 0.19 / (jnp.sqrt(new_second / 0.0975) + 1e-08)).astype(BF16)
    new_first = lax.dynamic_slice_in_dim(new_first, core * half, half, 0)
    new_second = lax.dynamic_slice_in_dim(new_second, core * half, half, 0)

    back = jnp.einsum("mn,zcn->zmc", update, basis_z, preferred_element_type=F32).astype(BF16)
    back = back.reshape(n_z, n_dp, sub, cols).transpose(1, 0, 2, 3)
    back = jnp.sum(exchange(back, DP).astype(F32), axis=0).astype(BF16)
    packed = exchange(jnp.concatenate([to_tiles(back), gram], axis=1), "z")
    back = from_tiles(packed[:, : 2 * sub], cols)
    left_gram = jnp.sum(packed[:, 2 * sub :].astype(F32), axis=0)
    back = exchange(jnp.broadcast_to(back[None], (n_dp, n_z, sub, cols)), DP)
    direction = jnp.dot(
        basis_p.reshape(rows, n_dp * rows),
        back.reshape(n_dp * rows, cols),
        preferred_element_type=F32,
    )
    return (left_gram.T, new_first.T, new_second.T, direction)


def solution(mesh):
    n_dp, n_col = mesh.shape["dp"], mesh.shape["col"]
    side = int(round(n_dp**0.5))
    fine = Mesh(
        mesh.devices.reshape(side, side, n_col // 2, 2), ("y", "x", "z", "core")
    )
    dp, col = ("y", "x"), ("z", "core")
    in_specs = (P(dp, None, col), P(dp, None), P(col, dp), P(dp, col), P(dp, col))
    out_specs = (P(dp, col), P(dp, col), P(dp, col), P(dp, col))
    return jax.shard_map(
        on_device, mesh=fine, in_specs=in_specs, out_specs=out_specs, check_vma=False
    )
```

```python
import jax
import jax.numpy as jnp
from jax import lax
from jax.sharding import Mesh, PartitionSpec as P

D = 7168
DP = ("y", "x")
F32 = jnp.float32
BF16 = jnp.bfloat16
LANES = 128


def exchange(chunks, axes):
    return lax.all_to_all(chunks, axes, 0, 0, tiled=True)


def swap_cores(block):
    return lax.ppermute(block, "core", [(0, 1), (1, 0)])


def to_tiles(block):
    z, sub, cols = block.shape
    block = jnp.pad(block, ((0, 0), (0, 0), (0, 2 * LANES - cols)))
    return block.reshape(z, sub, 2, LANES).transpose(0, 2, 1, 3).reshape(z, 2 * sub, LANES)


def from_tiles(block, cols):
    z, rows, _ = block.shape
    block = block.reshape(z, 2, rows // 2, LANES).transpose(0, 2, 1, 3)
    return block.reshape(z, rows // 2, 2 * LANES)[:, :, :cols]


def on_device(grad_parts, left_basis, right_basis, first_moment, second_moment):
    rows = left_basis.shape[0]
    cols = right_basis.shape[0]
    turns = right_basis.shape[1]
    n_dp = left_basis.shape[1] // rows
    n_z = lax.axis_size("z")
    sub = rows // n_dp
    half = rows // 2
    core = lax.axis_index("core")

    def both(block):
        theirs = swap_cores(block)
        return jnp.where(core == 0, jnp.stack([block, theirs]), jnp.stack([theirs, block]))

    basis_z = lax.all_gather(right_basis, "z", axis=0, tiled=False)

    parts = grad_parts[0].T.reshape(cols, n_dp, rows).transpose(1, 0, 2)
    grad_t = jnp.sum(exchange(parts, DP).astype(F32), axis=0).astype(BF16)

    basis_p = (
        left_basis.reshape(rows, n_z, n_dp, sub).transpose(0, 2, 1, 3).reshape(rows, n_dp, rows)
    )
    left_term = lax.dot_general(
        basis_p, grad_t, (((0,), (1,)), ((), ())), preferred_element_type=F32
    )
    turned, moments = lax.optimization_barrier(
        (
            exchange(left_term.astype(BF16), DP),
            both(jnp.stack([first_moment.T, second_moment.T])),
        )
    )
    turned = jnp.sum(turned.astype(F32), axis=0).astype(BF16).reshape(n_z, sub, cols)

    turned, grad_here = lax.optimization_barrier((turned, grad_t))
    turned, grad_all = lax.optimization_barrier(
        (exchange(turned, "z"), lax.all_gather(grad_here, DP, axis=0, tiled=False))
    )
    turned = turned.transpose(1, 0, 2).reshape(1, sub, n_z * cols)
    turned = exchange(jnp.broadcast_to(turned, (n_dp, sub, n_z * cols)), DP)

    gram = lax.dot_general(
        grad_all, grad_t, (((1,), (0,)), ((), ())), preferred_element_type=F32
    ).reshape(n_z, 2, half, rows) / D
    mine = lax.dynamic_index_in_dim(gram, core, 1, keepdims=False)
    other = lax.dynamic_index_in_dim(gram, 1 - core, 1, keepdims=False)
    gram = (mine + swap_cores(other.astype(BF16)).astype(F32)).astype(BF16)
    turned, gram = lax.optimization_barrier((turned, gram))

    basis_z = basis_z.reshape(n_z * cols, turns)
    rotated = jnp.dot(
        turned.reshape(rows, n_z * cols), basis_z, preferred_element_type=F32
    )
    rotated = rotated + swap_cores(rotated.astype(BF16)).astype(F32)
    new_first = 0.9 * moments[:, 0].reshape(rows, turns) + 0.1 * rotated
    new_second = 0.95 * moments[:, 1].reshape(rows, turns) + 0.05 * rotated * rotated
    update = (new_first / 0.19 / (jnp.sqrt(new_second / 0.0975) + 1e-08)).astype(BF16)
    new_first = lax.dynamic_slice_in_dim(new_first, core * half, half, 0)
    new_second = lax.dynamic_slice_in_dim(new_second, core * half, half, 0)

    back = lax.dot_general(
        update, basis_z, (((1,), (1,)), ((), ())), preferred_element_type=F32
    ).astype(BF16)
    back = exchange(back.reshape(n_dp, sub, n_z * cols), DP)
    back = jnp.sum(back.astype(F32), axis=0).astype(BF16)
    back = back.reshape(sub, n_z, cols).transpose(1, 0, 2)
    packed = exchange(jnp.concatenate([to_tiles(back), gram], axis=1), "z")
    back = from_tiles(packed[:, : 2 * sub], cols)
    left_gram = jnp.sum(packed[:, 2 * sub :].astype(F32), axis=0)
    back = back.reshape(rows, cols).T
    back = exchange(jnp.broadcast_to(back[None], (n_dp, cols, rows)), DP)
    direction = lax.dot_general(
        basis_p, back, (((1, 2), (0, 2)), ((), ())), preferred_element_type=F32
    )
    return (left_gram.T, new_first.T, new_second.T, direction)


def solution(mesh):
    n_dp, n_col = mesh.shape["dp"], mesh.shape["col"]
    side = int(round(n_dp**0.5))
    fine = Mesh(
        mesh.devices.reshape(side, side, n_col // 2, 2), ("y", "x", "z", "core")
    )
    dp, col = ("y", "x"), ("z", "core")
    in_specs = (P(dp, None, col), P(dp, None), P(col, dp), P(dp, col), P(dp, col))
    out_specs = (P(dp, col), P(dp, col), P(dp, col), P(dp, col))
    return jax.shard_map(
        on_device, mesh=fine, in_specs=in_specs, out_specs=out_specs, check_vma=False
    )
```

```python
import jax
import jax.numpy as jnp
from jax import lax
from jax.sharding import Mesh, PartitionSpec as P

D = 7168
DP = ("y", "x")
Z = ("zh", "zl")
F32 = jnp.float32
BF16 = jnp.bfloat16


def exchange(chunks, axes):
    return lax.all_to_all(chunks, axes, 0, 0, tiled=True)


def swap(block, axis):
    return lax.ppermute(block, axis, [(0, 1), (1, 0)])


def both(block, axis):
    theirs = swap(block, axis)
    return jnp.where(
        lax.axis_index(axis) == 0, jnp.stack([block, theirs]), jnp.stack([theirs, block])
    )


def on_device(grad_parts, left_basis, right_basis, first_moment, second_moment):
    rows = left_basis.shape[0]
    cols = right_basis.shape[0]
    turns = right_basis.shape[1]
    n_dp = left_basis.shape[1] // rows
    n_zh = lax.axis_size("zh")
    n_z = 2 * n_zh
    sub = rows // n_zh
    half = rows // 2
    core = lax.axis_index("core")
    block = n_dp * sub
    depth = n_zh * cols

    basis_z = lax.all_gather(right_basis, "zh", axis=0, tiled=True)

    parts = grad_parts[0].T.reshape(cols, n_dp, rows).transpose(1, 0, 2)
    grad_t = jnp.sum(exchange(parts, DP).astype(F32), axis=0).astype(BF16)

    basis_p = (
        left_basis.reshape(rows, n_zh, n_dp, sub).transpose(0, 2, 1, 3).reshape(rows, n_dp, rows)
    )
    left_term = lax.dot_general(
        basis_p, grad_t, (((0,), (1,)), ((), ())), preferred_element_type=F32
    )
    moments = both(both(jnp.stack([first_moment.T, second_moment.T]), "core"), "zl")
    turned, moments = lax.optimization_barrier((exchange(left_term.astype(BF16), DP), moments))
    turned = jnp.sum(turned.astype(F32), axis=0).astype(BF16).reshape(n_zh, sub, cols)
    turned = exchange(turned, "zh")
    turned = turned.transpose(1, 0, 2).reshape(1, sub, depth)
    turned = exchange(jnp.broadcast_to(turned, (n_dp, sub, depth)), DP)

    turned, grad_here = lax.optimization_barrier((turned, grad_t))
    grad_all = exchange(jnp.broadcast_to(grad_here[None], (n_dp, cols, rows)), DP)

    rotated = jnp.dot(turned.reshape(block, depth), basis_z, preferred_element_type=F32)
    rotated = rotated + swap(rotated.astype(BF16), "core").astype(F32)
    rotated = rotated + swap(rotated.astype(BF16), "zl").astype(F32)
    new_first = 0.9 * moments[:, :, 0].reshape(block, turns) + 0.1 * rotated
    new_second = 0.95 * moments[:, :, 1].reshape(block, turns) + 0.05 * rotated * rotated
    update = (new_first / 0.19 / (jnp.sqrt(new_second / 0.0975) + 1e-08)).astype(BF16)
    mine = (2 * lax.axis_index("zl") + core) * half
    new_first = lax.dynamic_slice_in_dim(new_first, mine, half, 0)
    new_second = lax.dynamic_slice_in_dim(new_second, mine, half, 0)
    back = lax.dot_general(
        update, basis_z, (((1,), (1,)), ((), ())), preferred_element_type=F32
    ).astype(BF16)
    back, grad_all = lax.optimization_barrier((back, grad_all))
    back = exchange(back.reshape(n_dp, sub, depth), DP)

    gram = lax.dot_general(
        grad_all, grad_t, (((1,), (0,)), ((), ())), preferred_element_type=F32
    ).reshape(n_z, 2, half, rows) / D
    mine = lax.dynamic_index_in_dim(gram, core, 1, keepdims=False)
    other = lax.dynamic_index_in_dim(gram, 1 - core, 1, keepdims=False)
    gram = (mine + swap(other.astype(BF16), "core").astype(F32)).astype(BF16)
    back, gram = lax.optimization_barrier((back, gram))

    back = jnp.sum(back.astype(F32), axis=0).astype(BF16)
    back = exchange(back.reshape(sub, n_zh, cols).transpose(1, 0, 2), "zh")
    back, gram = lax.optimization_barrier((back, gram))
    left_gram = jnp.sum(exchange(gram, Z).astype(F32), axis=0)
    back = lax.all_gather(back.reshape(rows, cols).T, DP, axis=0, tiled=False)
    direction = lax.dot_general(
        basis_p, back, (((1, 2), (0, 2)), ((), ())), preferred_element_type=F32
    )
    return (left_gram.T, new_first.T, new_second.T, direction)


def solution(mesh):
    n_dp, n_col = mesh.shape["dp"], mesh.shape["col"]
    side = int(round(n_dp**0.5))
    fine = Mesh(
        mesh.devices.reshape(side, side, n_col // 4, 2, 2), ("y", "x", "zh", "zl", "core")
    )
    dp, col = ("y", "x"), ("zh", "zl", "core")
    in_specs = (P(dp, None, col), P(dp, None), P(col, dp), P(dp, col), P(dp, col))
    out_specs = (P(dp, col), P(dp, col), P(dp, col), P(dp, col))
    return jax.shard_map(
        on_device, mesh=fine, in_specs=in_specs, out_specs=out_specs, check_vma=False
    )
```

```python
import jax
import jax.numpy as jnp
from jax import lax
from jax.sharding import Mesh, PartitionSpec as P

D = 7168
DP = ("y", "x")
F32 = jnp.float32
BF16 = jnp.bfloat16
LANES = 128


def exchange(chunks, axes):
    return lax.all_to_all(chunks, axes, 0, 0, tiled=True)


def swap_cores(block):
    return lax.ppermute(block, "core", [(0, 1), (1, 0)])


def to_tiles(block):
    z, sub, cols = block.shape
    block = jnp.pad(block, ((0, 0), (0, 0), (0, 2 * LANES - cols)))
    return block.reshape(z, sub, 2, LANES).transpose(0, 2, 1, 3).reshape(z, 2 * sub, LANES)


def from_tiles(block, cols):
    z, rows, _ = block.shape
    block = block.reshape(z, 2, rows // 2, LANES).transpose(0, 2, 1, 3)
    return block.reshape(z, rows // 2, 2 * LANES)[:, :, :cols]


def on_device(grad_parts, left_basis, right_basis, first_moment, second_moment):
    rows = left_basis.shape[0]
    cols = right_basis.shape[0]
    turns = right_basis.shape[1]
    n_dp = left_basis.shape[1] // rows
    n_z = lax.axis_size("z")
    sub = rows // n_dp
    half = rows // 2
    core = lax.axis_index("core")

    def both(block):
        theirs = swap_cores(block)
        return jnp.where(core == 0, jnp.stack([block, theirs]), jnp.stack([theirs, block]))

    basis_z = lax.all_gather(right_basis, "z", axis=0, tiled=False)

    parts = grad_parts[0].T.reshape(cols, n_dp, rows).transpose(1, 0, 2)
    grad_t = jnp.sum(exchange(parts, DP).astype(F32), axis=0).astype(BF16)

    basis_p = (
        left_basis.reshape(rows, n_z, n_dp, sub).transpose(0, 2, 1, 3).reshape(rows, n_dp, rows)
    )
    left_term = lax.dot_general(
        basis_p, grad_t, (((0,), (1,)), ((), ())), preferred_element_type=F32
    )
    turned, moments = lax.optimization_barrier(
        (
            exchange(left_term.astype(BF16), DP),
            both(jnp.stack([first_moment.T, second_moment.T])),
        )
    )
    turned = jnp.sum(turned.astype(F32), axis=0).astype(BF16).reshape(n_z, sub, cols)

    turned = exchange(turned, "z")
    turned = turned.transpose(1, 0, 2).reshape(1, sub, n_z * cols)
    turned = exchange(jnp.broadcast_to(turned, (n_dp, sub, n_z * cols)), DP)

    turned, grad_here = lax.optimization_barrier((turned, grad_t))
    grad_all = exchange(jnp.broadcast_to(grad_here[None], (n_dp, cols, rows)), DP)

    basis_z = basis_z.reshape(n_z * cols, turns)
    rotated = jnp.dot(
        turned.reshape(rows, n_z * cols), basis_z, preferred_element_type=F32
    )
    rotated = rotated + swap_cores(rotated.astype(BF16)).astype(F32)
    new_first = 0.9 * moments[:, 0].reshape(rows, turns) + 0.1 * rotated
    new_second = 0.95 * moments[:, 1].reshape(rows, turns) + 0.05 * rotated * rotated
    update = (new_first / 0.19 / (jnp.sqrt(new_second / 0.0975) + 1e-08)).astype(BF16)
    new_first = lax.dynamic_slice_in_dim(new_first, core * half, half, 0)
    new_second = lax.dynamic_slice_in_dim(new_second, core * half, half, 0)

    back = lax.dot_general(
        update, basis_z, (((1,), (1,)), ((), ())), preferred_element_type=F32
    ).astype(BF16)
    back, grad_all = lax.optimization_barrier((back, grad_all))
    back = exchange(back.reshape(n_dp, sub, n_z * cols), DP)

    gram = lax.dot_general(
        grad_all, grad_t, (((1,), (0,)), ((), ())), preferred_element_type=F32
    ).reshape(n_z, 2, half, rows) / D
    mine = lax.dynamic_index_in_dim(gram, core, 1, keepdims=False)
    other = lax.dynamic_index_in_dim(gram, 1 - core, 1, keepdims=False)
    gram = (mine + swap_cores(other.astype(BF16)).astype(F32)).astype(BF16)
    back, gram = lax.optimization_barrier((back, gram))

    back = jnp.sum(back.astype(F32), axis=0).astype(BF16)
    back = back.reshape(sub, n_z, cols).transpose(1, 0, 2)
    packed = exchange(jnp.concatenate([to_tiles(back), gram], axis=1), "z")
    back = from_tiles(packed[:, : 2 * sub], cols)
    left_gram = jnp.sum(packed[:, 2 * sub :].astype(F32), axis=0)
    back = back.reshape(rows, cols).T
    back = exchange(jnp.broadcast_to(back[None], (n_dp, cols, rows)), DP)
    direction = lax.dot_general(
        basis_p, back, (((1, 2), (0, 2)), ((), ())), preferred_element_type=F32
    )
    return (left_gram.T, new_first.T, new_second.T, direction)


def solution(mesh):
    n_dp, n_col = mesh.shape["dp"], mesh.shape["col"]
    side = int(round(n_dp**0.5))
    fine = Mesh(
        mesh.devices.reshape(side, side, n_col // 2, 2), ("y", "x", "z", "core")
    )
    dp, col = ("y", "x"), ("z", "core")
    in_specs = (P(dp, None, col), P(dp, None), P(col, dp), P(dp, col), P(dp, col))
    out_specs = (P(dp, col), P(dp, col), P(dp, col), P(dp, col))
    return jax.shard_map(
        on_device, mesh=fine, in_specs=in_specs, out_specs=out_specs, check_vma=False
    )
```

```python
import jax
import jax.numpy as jnp
from jax import lax
from jax.sharding import Mesh, PartitionSpec as P

D = 7168
DP = ("y", "x")
F32 = jnp.float32
BF16 = jnp.bfloat16
LANES = 128


def exchange(chunks, axes):
    return lax.all_to_all(chunks, axes, 0, 0, tiled=True)


def swap_cores(block):
    return lax.ppermute(block, "core", [(0, 1), (1, 0)])


def to_tiles(block):
    z, sub, cols = block.shape
    block = jnp.pad(block, ((0, 0), (0, 0), (0, 2 * LANES - cols)))
    return block.reshape(z, sub, 2, LANES).transpose(0, 2, 1, 3).reshape(z, 2 * sub, LANES)


def from_tiles(block, cols):
    z, rows, _ = block.shape
    block = block.reshape(z, 2, rows // 2, LANES).transpose(0, 2, 1, 3)
    return block.reshape(z, rows // 2, 2 * LANES)[:, :, :cols]


def on_device(grad_parts, left_basis, right_basis, first_moment, second_moment):
    rows = left_basis.shape[0]
    cols = right_basis.shape[0]
    turns = right_basis.shape[1]
    n_dp = left_basis.shape[1] // rows
    n_z = lax.axis_size("z")
    sub = rows // n_dp
    half = rows // 2
    core = lax.axis_index("core")

    def both(block):
        theirs = swap_cores(block)
        return jnp.where(core == 0, jnp.stack([block, theirs]), jnp.stack([theirs, block]))

    basis_z = lax.all_gather(right_basis, "z", axis=0, tiled=False)

    parts = grad_parts[0].T.reshape(cols, n_dp, rows).transpose(1, 0, 2)
    parts, moments = lax.optimization_barrier(
        (exchange(parts, DP), both(jnp.stack([first_moment.T, second_moment.T])))
    )
    grad_t = jnp.sum(parts.astype(F32), axis=0).astype(BF16)

    basis_p = (
        left_basis.reshape(rows, n_z, n_dp, sub).transpose(0, 2, 1, 3).reshape(rows, n_dp, rows)
    )
    left_term = lax.dot_general(
        basis_p, grad_t, (((0,), (1,)), ((), ())), preferred_element_type=F32
    )
    turned, grad_x = lax.optimization_barrier(
        (exchange(left_term.astype(BF16), DP), lax.all_gather(grad_t, "x", axis=0, tiled=False))
    )
    turned = jnp.sum(turned.astype(F32), axis=0).astype(BF16).reshape(n_z, sub, cols)
    turned, grad_x = lax.optimization_barrier((turned, grad_x))
    turned, grad_all = lax.optimization_barrier(
        (exchange(turned, "z"), lax.all_gather(grad_x, "y", axis=0, tiled=True))
    )
    turned = turned.transpose(1, 0, 2).reshape(1, sub, n_z * cols)
    turned = exchange(jnp.broadcast_to(turned, (n_dp, sub, n_z * cols)), DP)

    gram = lax.dot_general(
        grad_all, grad_t, (((1,), (0,)), ((), ())), preferred_element_type=F32
    ).reshape(n_z, 2, half, rows) / D
    mine = lax.dynamic_index_in_dim(gram, core, 1, keepdims=False)
    other = lax.dynamic_index_in_dim(gram, 1 - core, 1, keepdims=False)
    gram = (mine + swap_cores(other.astype(BF16)).astype(F32)).astype(BF16)
    turned, gram = lax.optimization_barrier((turned, gram))

    basis_z = basis_z.reshape(n_z * cols, turns)
    rotated = jnp.dot(
        turned.reshape(rows, n_z * cols), basis_z, preferred_element_type=F32
    )
    rotated = rotated + swap_cores(rotated.astype(BF16)).astype(F32)
    new_first = 0.9 * moments[:, 0].reshape(rows, turns) + 0.1 * rotated
    new_second = 0.95 * moments[:, 1].reshape(rows, turns) + 0.05 * rotated * rotated
    update = (new_first / 0.19 / (jnp.sqrt(new_second / 0.0975) + 1e-08)).astype(BF16)
    new_first = lax.dynamic_slice_in_dim(new_first, core * half, half, 0)
    new_second = lax.dynamic_slice_in_dim(new_second, core * half, half, 0)

    back = lax.dot_general(
        update, basis_z, (((1,), (1,)), ((), ())), preferred_element_type=F32
    ).astype(BF16)
    back = exchange(back.reshape(n_dp, sub, n_z * cols), DP)
    back = jnp.sum(back.astype(F32), axis=0).astype(BF16)
    back = back.reshape(sub, n_z, cols).transpose(1, 0, 2)
    packed = exchange(jnp.concatenate([to_tiles(back), gram], axis=1), "z")
    back = from_tiles(packed[:, : 2 * sub], cols)
    left_gram = jnp.sum(packed[:, 2 * sub :].astype(F32), axis=0)
    back = back.reshape(rows, cols).T
    back = exchange(jnp.broadcast_to(back[None], (n_dp, cols, rows)), DP)
    direction = lax.dot_general(
        basis_p, back, (((1, 2), (0, 2)), ((), ())), preferred_element_type=F32
    )
    return (left_gram.T, new_first.T, new_second.T, direction)


def solution(mesh):
    n_dp, n_col = mesh.shape["dp"], mesh.shape["col"]
    side = int(round(n_dp**0.5))
    fine = Mesh(
        mesh.devices.reshape(side, side, n_col // 2, 2), ("y", "x", "z", "core")
    )
    dp, col = ("y", "x"), ("z", "core")
    in_specs = (P(dp, None, col), P(dp, None), P(col, dp), P(dp, col), P(dp, col))
    out_specs = (P(dp, col), P(dp, col), P(dp, col), P(dp, col))
    return jax.shard_map(
        on_device, mesh=fine, in_specs=in_specs, out_specs=out_specs, check_vma=False
    )
```

```python
import jax
import jax.numpy as jnp
from jax import lax
from jax.experimental import pallas as pl
from jax.experimental.pallas import tpu as pltpu
from jax.sharding import Mesh, PartitionSpec as P

D = 7168
DP = ("y", "x")
F32 = jnp.float32
BF16 = jnp.bfloat16
LANES = 128


def exchange(chunks, axes):
    return lax.all_to_all(chunks, axes, 0, 0, tiled=True)


def swap_cores(block):
    return lax.ppermute(block, "core", [(0, 1), (1, 0)])


def to_tiles(block):
    z, sub, cols = block.shape
    block = jnp.pad(block, ((0, 0), (0, 0), (0, 2 * LANES - cols)))
    return block.reshape(z, sub, 2, LANES).transpose(0, 2, 1, 3).reshape(z, 2 * sub, LANES)


def from_tiles(block, cols):
    z, rows, _ = block.shape
    block = block.reshape(z, 2, rows // 2, LANES).transpose(0, 2, 1, 3)
    return block.reshape(z, rows // 2, 2 * LANES)[:, :, :cols]


def rotate_kernel(turned_ref, basis_ref, total_ref, send_ref):
    total = jnp.dot(turned_ref[...], basis_ref[...], preferred_element_type=F32)
    total_ref[...] = total
    send_ref[...] = total.astype(BF16)


def vmem():
    return pl.BlockSpec(memory_space=pltpu.VMEM)


def rotate(turned, basis):
    rows, depth = turned.shape
    turns = basis.shape[1]
    return pl.pallas_call(
        rotate_kernel,
        in_specs=[vmem(), vmem()],
        out_specs=[vmem(), vmem()],
        out_shape=[
            jax.ShapeDtypeStruct((rows, turns), F32),
            jax.ShapeDtypeStruct((rows, turns), BF16),
        ],
        compiler_params=pltpu.CompilerParams(vmem_limit_bytes=32 * 2**20),
        cost_estimate=pl.CostEstimate(
            flops=2 * rows * depth * turns,
            bytes_accessed=2 * depth * (rows + turns) + 6 * rows * turns,
            transcendentals=0,
        ),
    )(turned, basis)


def update_kernel(
    core_ref, total_ref, theirs_ref, moments_ref, basis_ref, first_ref, second_ref, back_ref
):
    half = first_ref.shape[0]
    updates = []
    for i in range(2):
        rows = slice(i * half, (i + 1) * half)
        rotated = total_ref[rows, :] + theirs_ref[rows, :].astype(F32)
        first = 0.9 * moments_ref[i, 0] + 0.1 * rotated
        second = 0.95 * moments_ref[i, 1] + 0.05 * rotated * rotated
        updates.append(first / 0.19 / (jnp.sqrt(second / 0.0975) + 1e-08))

        @pl.when(core_ref[0] == i)
        def _():
            first_ref[...] = first
            second_ref[...] = second

    update = jnp.concatenate(updates, axis=0).astype(BF16)
    step = 512
    for i in range(basis_ref.shape[0] // step):
        part = slice(i * step, (i + 1) * step)
        back_ref[:, part] = lax.dot_general(
            update, basis_ref[part, :], (((1,), (1,)), ((), ())), preferred_element_type=F32
        ).astype(BF16)


def update_and_back(core, total, theirs, moments, basis):
    rows, turns = total.shape
    depth = basis.shape[0]
    half = rows // 2
    return pl.pallas_call(
        update_kernel,
        in_specs=[pl.BlockSpec(memory_space=pltpu.SMEM)] + [vmem()] * 4,
        out_specs=[vmem()] * 3,
        out_shape=[
            jax.ShapeDtypeStruct((half, turns), F32),
            jax.ShapeDtypeStruct((half, turns), F32),
            jax.ShapeDtypeStruct((rows, depth), BF16),
        ],
        compiler_params=pltpu.CompilerParams(vmem_limit_bytes=32 * 2**20),
        cost_estimate=pl.CostEstimate(
            flops=2 * rows * depth * turns,
            bytes_accessed=2 * depth * (rows + turns) + 22 * rows * turns,
            transcendentals=rows * turns,
        ),
    )(core.reshape(1), total, theirs, moments, basis)


def on_device(grad_parts, left_basis, right_basis, first_moment, second_moment):
    rows = left_basis.shape[0]
    cols = right_basis.shape[0]
    turns = right_basis.shape[1]
    n_dp = left_basis.shape[1] // rows
    n_z = lax.axis_size("z")
    sub = rows // n_dp
    half = rows // 2
    core = lax.axis_index("core")

    def both(block):
        theirs = swap_cores(block)
        return jnp.where(core == 0, jnp.stack([block, theirs]), jnp.stack([theirs, block]))

    basis_z = lax.all_gather(right_basis, "z", axis=0, tiled=False)

    parts, moments = lax.optimization_barrier(
        (
            exchange(grad_parts[0].reshape(n_dp, rows, cols), DP),
            both(jnp.stack([first_moment.T, second_moment.T])),
        )
    )
    grad_t = jnp.sum(parts.astype(F32), axis=0).astype(BF16).T

    basis_p = (
        left_basis.reshape(rows, n_z, n_dp, sub).transpose(0, 2, 1, 3).reshape(rows, n_dp, rows)
    )
    left_term = lax.dot_general(
        basis_p, grad_t, (((0,), (1,)), ((), ())), preferred_element_type=F32
    )
    turned = exchange(left_term.astype(BF16), DP)
    turned = jnp.sum(turned.astype(F32), axis=0).astype(BF16).reshape(n_z, sub, cols)

    turned, copies = lax.optimization_barrier(
        (exchange(turned, "z"), jnp.broadcast_to(grad_t[None], (n_dp, cols, rows)))
    )
    turned = turned.transpose(1, 0, 2).reshape(1, sub, n_z * cols)
    turned = exchange(jnp.broadcast_to(turned, (n_dp, sub, n_z * cols)), DP)

    turned, copies = lax.optimization_barrier((turned, copies))
    grad_all = exchange(copies, DP)

    basis_z = basis_z.reshape(n_z * cols, turns)
    total, send = rotate(turned.reshape(rows, n_z * cols), basis_z)
    new_first, new_second, back = update_and_back(
        core, total, swap_cores(send), moments, basis_z
    )
    back, grad_all = lax.optimization_barrier((back, grad_all))
    back = exchange(back.reshape(n_dp, sub, n_z * cols), DP)

    gram = lax.dot_general(
        grad_all, grad_t, (((1,), (0,)), ((), ())), preferred_element_type=F32
    ).reshape(n_z, 2, half, rows) / D
    mine = lax.dynamic_index_in_dim(gram, core, 1, keepdims=False)
    other = lax.dynamic_index_in_dim(gram, 1 - core, 1, keepdims=False)
    gram = mine + swap_cores(other.astype(BF16)).astype(F32)
    quarter = half // 2
    gram = gram.reshape(n_z, 2, quarter, rows)
    low = lax.axis_index("z") % 2
    mine = lax.dynamic_index_in_dim(gram, low, 1, keepdims=False)
    other = lax.dynamic_index_in_dim(gram, 1 - low, 1, keepdims=False)
    pairs = [(i, i ^ 1) for i in range(n_z)]
    gram = mine + lax.ppermute(other.astype(BF16), "z", pairs).astype(F32)
    gram = gram.astype(BF16)
    back, gram = lax.optimization_barrier((back, gram))

    back = jnp.sum(back.astype(F32), axis=0).astype(BF16)
    back = back.reshape(sub, n_z, cols).transpose(1, 0, 2)
    packed = exchange(jnp.concatenate([to_tiles(back), gram], axis=1), "z")
    back = from_tiles(packed[:, : 2 * sub], cols)
    left_gram = packed[:, 2 * sub :].reshape(n_z // 2, half, rows)
    left_gram = jnp.sum(left_gram.astype(F32), axis=0)
    back = back.reshape(rows, cols).T
    back = exchange(jnp.broadcast_to(back[None], (n_dp, cols, rows)), DP)
    direction = lax.dot_general(
        basis_p, back, (((1, 2), (0, 2)), ((), ())), preferred_element_type=F32
    )
    return (left_gram.T, new_first.T, new_second.T, direction)


def solution(mesh):
    n_dp, n_col = mesh.shape["dp"], mesh.shape["col"]
    side = int(round(n_dp**0.5))
    fine = Mesh(
        mesh.devices.reshape(side, side, n_col // 2, 2), ("y", "x", "z", "core")
    )
    dp, col = ("y", "x"), ("z", "core")
    in_specs = (P(dp, None, col), P(dp, None), P(col, dp), P(dp, col), P(dp, col))
    out_specs = (P(dp, col), P(dp, col), P(dp, col), P(dp, col))
    return jax.shard_map(
        on_device, mesh=fine, in_specs=in_specs, out_specs=out_specs, check_vma=False
    )
```

```python
import jax
import jax.numpy as jnp
from jax import lax
from jax.experimental import pallas as pl
from jax.experimental.pallas import tpu as pltpu
from jax.sharding import Mesh, PartitionSpec as P

D = 7168
DP = ("y", "x")
F32 = jnp.float32
BF16 = jnp.bfloat16
LANES = 128


def exchange(chunks, axes):
    return lax.all_to_all(chunks, axes, 0, 0, tiled=True)


def swap_cores(block):
    return lax.ppermute(block, "core", [(0, 1), (1, 0)])


def to_tiles(block):
    z, sub, cols = block.shape
    block = jnp.pad(block, ((0, 0), (0, 0), (0, 2 * LANES - cols)))
    return block.reshape(z, sub, 2, LANES).transpose(0, 2, 1, 3).reshape(z, 2 * sub, LANES)


def from_tiles(block, cols):
    z, rows, _ = block.shape
    block = block.reshape(z, 2, rows // 2, LANES).transpose(0, 2, 1, 3)
    return block.reshape(z, rows // 2, 2 * LANES)[:, :, :cols]


def rotate_kernel(turned_ref, basis_ref, total_ref, send_ref):
    total = jnp.dot(turned_ref[...], basis_ref[...], preferred_element_type=F32)
    total_ref[...] = total
    send_ref[...] = total.astype(BF16)


def vmem():
    return pl.BlockSpec(memory_space=pltpu.VMEM)


def rotate(turned, basis):
    rows, depth = turned.shape
    turns = basis.shape[1]
    return pl.pallas_call(
        rotate_kernel,
        in_specs=[vmem(), vmem()],
        out_specs=[vmem(), vmem()],
        out_shape=[
            jax.ShapeDtypeStruct((rows, turns), F32),
            jax.ShapeDtypeStruct((rows, turns), BF16),
        ],
        compiler_params=pltpu.CompilerParams(vmem_limit_bytes=32 * 2**20),
        cost_estimate=pl.CostEstimate(
            flops=2 * rows * depth * turns,
            bytes_accessed=2 * depth * (rows + turns) + 6 * rows * turns,
            transcendentals=0,
        ),
    )(turned, basis)


def update_kernel(
    core_ref, total_ref, theirs_ref, moments_ref, basis_ref, first_ref, second_ref, back_ref
):
    half = first_ref.shape[0]
    updates = []
    for i in range(2):
        rows = slice(i * half, (i + 1) * half)
        rotated = total_ref[rows, :] + theirs_ref[rows, :].astype(F32)
        first = 0.9 * moments_ref[i, 0] + 0.1 * rotated
        second = 0.95 * moments_ref[i, 1] + 0.05 * rotated * rotated
        updates.append(first / 0.19 / (jnp.sqrt(second / 0.0975) + 1e-08))

        @pl.when(core_ref[0] == i)
        def _():
            first_ref[...] = first
            second_ref[...] = second

    update = jnp.concatenate(updates, axis=0).astype(BF16)
    step = 512
    for i in range(basis_ref.shape[0] // step):
        part = slice(i * step, (i + 1) * step)
        back_ref[:, part] = lax.dot_general(
            update, basis_ref[part, :], (((1,), (1,)), ((), ())), preferred_element_type=F32
        ).astype(BF16)


def update_and_back(core, total, theirs, moments, basis):
    rows, turns = total.shape
    depth = basis.shape[0]
    half = rows // 2
    return pl.pallas_call(
        update_kernel,
        in_specs=[pl.BlockSpec(memory_space=pltpu.SMEM)] + [vmem()] * 4,
        out_specs=[vmem()] * 3,
        out_shape=[
            jax.ShapeDtypeStruct((half, turns), F32),
            jax.ShapeDtypeStruct((half, turns), F32),
            jax.ShapeDtypeStruct((rows, depth), BF16),
        ],
        compiler_params=pltpu.CompilerParams(vmem_limit_bytes=32 * 2**20),
        cost_estimate=pl.CostEstimate(
            flops=2 * rows * depth * turns,
            bytes_accessed=2 * depth * (rows + turns) + 22 * rows * turns,
            transcendentals=rows * turns,
        ),
    )(core.reshape(1), total, theirs, moments, basis)


def on_device(grad_parts, left_basis, right_basis, first_moment, second_moment):
    rows = left_basis.shape[0]
    cols = right_basis.shape[0]
    turns = right_basis.shape[1]
    n_dp = left_basis.shape[1] // rows
    n_z = lax.axis_size("z")
    sub = rows // n_dp
    half = rows // 2
    core = lax.axis_index("core")

    def both(block):
        theirs = swap_cores(block)
        return jnp.where(core == 0, jnp.stack([block, theirs]), jnp.stack([theirs, block]))

    basis_z = lax.all_gather(right_basis, "z", axis=0, tiled=False)

    parts, moments = lax.optimization_barrier(
        (
            exchange(grad_parts[0].reshape(n_dp, rows, cols), DP),
            both(jnp.stack([first_moment.T, second_moment.T])),
        )
    )
    grad_t = jnp.sum(parts.astype(F32), axis=0).astype(BF16).T

    basis_p = (
        left_basis.reshape(rows, n_z, n_dp, sub).transpose(0, 2, 1, 3).reshape(rows, n_dp, rows)
    )
    left_term = lax.dot_general(
        basis_p, grad_t, (((0,), (1,)), ((), ())), preferred_element_type=F32
    )
    turned = exchange(left_term.astype(BF16), DP)
    turned = jnp.sum(turned.astype(F32), axis=0).astype(BF16).reshape(n_z, sub, cols)

    turned, copies = lax.optimization_barrier(
        (exchange(turned, "z"), jnp.broadcast_to(grad_t[None], (n_dp, cols, rows)))
    )
    turned = turned.transpose(1, 0, 2).reshape(1, sub, n_z * cols)
    turned = exchange(jnp.broadcast_to(turned, (n_dp, sub, n_z * cols)), DP)

    turned, copies = lax.optimization_barrier((turned, copies))
    grad_all = exchange(copies, DP)

    basis_z = basis_z.reshape(n_z * cols, turns)
    total, send = rotate(turned.reshape(rows, n_z * cols), basis_z)
    new_first, new_second, back = update_and_back(
        core, total, swap_cores(send), moments, basis_z
    )
    back, grad_all = lax.optimization_barrier((back, grad_all))
    back = exchange(back.reshape(n_dp, sub, n_z * cols), DP)

    gram = lax.dot_general(
        grad_all, grad_t, (((1,), (0,)), ((), ())), preferred_element_type=F32
    ).reshape(n_z, 4, half // 2, rows) / D
    low = lax.axis_index("z") % 2
    place = core * 2 + low
    mine = lax.dynamic_index_in_dim(gram, place, 1, keepdims=False)
    col = ("z", "core")
    for other, flip in ((place ^ 2, 1), (place ^ 1, 2), (place ^ 3, 3)):
        piece = lax.dynamic_index_in_dim(gram, other, 1, keepdims=False).astype(BF16)
        pairs = [(i, i ^ flip) for i in range(2 * n_z)]
        mine = mine + lax.ppermute(piece, col, pairs).astype(F32)
    gram = mine.astype(BF16)
    back, gram = lax.optimization_barrier((back, gram))

    back = jnp.sum(back.astype(F32), axis=0).astype(BF16)
    back = back.reshape(sub, n_z, cols).transpose(1, 0, 2)
    packed = exchange(jnp.concatenate([to_tiles(back), gram], axis=1), "z")
    back = from_tiles(packed[:, : 2 * sub], cols)
    left_gram = packed[:, 2 * sub :].reshape(n_z // 2, half, rows)
    left_gram = jnp.sum(left_gram.astype(F32), axis=0)
    back = back.reshape(rows, cols).T
    back = exchange(jnp.broadcast_to(back[None], (n_dp, cols, rows)), DP)
    direction = lax.dot_general(
        basis_p, back, (((1, 2), (0, 2)), ((), ())), preferred_element_type=F32
    )
    return (left_gram.T, new_first.T, new_second.T, direction)


def solution(mesh):
    n_dp, n_col = mesh.shape["dp"], mesh.shape["col"]
    side = int(round(n_dp**0.5))
    fine = Mesh(
        mesh.devices.reshape(side, side, n_col // 2, 2), ("y", "x", "z", "core")
    )
    dp, col = ("y", "x"), ("z", "core")
    in_specs = (P(dp, None, col), P(dp, None), P(col, dp), P(dp, col), P(dp, col))
    out_specs = (P(dp, col), P(dp, col), P(dp, col), P(dp, col))
    return jax.shard_map(
        on_device, mesh=fine, in_specs=in_specs, out_specs=out_specs, check_vma=False
    )
```

```python
import jax
import jax.numpy as jnp
from jax import lax
from jax.experimental import pallas as pl
from jax.experimental.pallas import tpu as pltpu
from jax.sharding import Mesh, PartitionSpec as P

D = 7168
DP = ("y", "x")
F32 = jnp.float32
BF16 = jnp.bfloat16
LANES = 128


def exchange(chunks, axes):
    return lax.all_to_all(chunks, axes, 0, 0, tiled=True)


def swap_cores(block):
    return lax.ppermute(block, "core", [(0, 1), (1, 0)])


def to_tiles(block):
    z, sub, cols = block.shape
    block = jnp.pad(block, ((0, 0), (0, 0), (0, 2 * LANES - cols)))
    return block.reshape(z, sub, 2, LANES).transpose(0, 2, 1, 3).reshape(z, 2 * sub, LANES)


def from_tiles(block, cols):
    z, rows, _ = block.shape
    block = block.reshape(z, 2, rows // 2, LANES).transpose(0, 2, 1, 3)
    return block.reshape(z, rows // 2, 2 * LANES)[:, :, :cols]


def rotate_kernel(turned_ref, basis_ref, total_ref, send_ref):
    total = jnp.dot(turned_ref[...], basis_ref[...], preferred_element_type=F32)
    total_ref[...] = total
    send_ref[...] = total.astype(BF16)


def vmem():
    return pl.BlockSpec(memory_space=pltpu.VMEM)


def rotate(turned, basis):
    rows, depth = turned.shape
    turns = basis.shape[1]
    return pl.pallas_call(
        rotate_kernel,
        in_specs=[vmem(), vmem()],
        out_specs=[vmem(), vmem()],
        out_shape=[
            jax.ShapeDtypeStruct((rows, turns), F32),
            jax.ShapeDtypeStruct((rows, turns), BF16),
        ],
        compiler_params=pltpu.CompilerParams(vmem_limit_bytes=32 * 2**20),
        cost_estimate=pl.CostEstimate(
            flops=2 * rows * depth * turns,
            bytes_accessed=2 * depth * (rows + turns) + 6 * rows * turns,
            transcendentals=0,
        ),
    )(turned, basis)


def update_kernel(
    core_ref, total_ref, theirs_ref, moments_ref, basis_ref, first_ref, second_ref, back_ref
):
    half = first_ref.shape[0]
    updates = []
    for i in range(2):
        rows = slice(i * half, (i + 1) * half)
        rotated = total_ref[rows, :] + theirs_ref[rows, :].astype(F32)
        first = 0.9 * moments_ref[i, 0] + 0.1 * rotated
        second = 0.95 * moments_ref[i, 1] + 0.05 * rotated * rotated
        updates.append(first / 0.19 / (jnp.sqrt(second / 0.0975) + 1e-08))

        @pl.when(core_ref[0] == i)
        def _():
            first_ref[...] = first
            second_ref[...] = second

    update = jnp.concatenate(updates, axis=0).astype(BF16)
    step = 512
    for i in range(basis_ref.shape[0] // step):
        part = slice(i * step, (i + 1) * step)
        back_ref[:, part] = lax.dot_general(
            update, basis_ref[part, :], (((1,), (1,)), ((), ())), preferred_element_type=F32
        ).astype(BF16)


def update_and_back(core, total, theirs, moments, basis):
    rows, turns = total.shape
    depth = basis.shape[0]
    half = rows // 2
    return pl.pallas_call(
        update_kernel,
        in_specs=[pl.BlockSpec(memory_space=pltpu.SMEM)] + [vmem()] * 4,
        out_specs=[vmem()] * 3,
        out_shape=[
            jax.ShapeDtypeStruct((half, turns), F32),
            jax.ShapeDtypeStruct((half, turns), F32),
            jax.ShapeDtypeStruct((rows, depth), BF16),
        ],
        compiler_params=pltpu.CompilerParams(vmem_limit_bytes=32 * 2**20),
        cost_estimate=pl.CostEstimate(
            flops=2 * rows * depth * turns,
            bytes_accessed=2 * depth * (rows + turns) + 22 * rows * turns,
            transcendentals=rows * turns,
        ),
    )(core.reshape(1), total, theirs, moments, basis)


def on_device(grad_parts, left_basis, right_basis, first_moment, second_moment):
    rows = left_basis.shape[0]
    cols = right_basis.shape[0]
    turns = right_basis.shape[1]
    n_dp = left_basis.shape[1] // rows
    n_z = lax.axis_size("z")
    sub = rows // n_dp
    half = rows // 2
    core = lax.axis_index("core")

    def both(block):
        theirs = swap_cores(block)
        return jnp.where(core == 0, jnp.stack([block, theirs]), jnp.stack([theirs, block]))

    basis_z = lax.all_gather(right_basis, "z", axis=0, tiled=False)

    parts, moments = lax.optimization_barrier(
        (
            exchange(grad_parts[0].reshape(n_dp, rows, cols), DP),
            both(jnp.stack([first_moment.T, second_moment.T])),
        )
    )
    grad_t = jnp.sum(parts.astype(F32), axis=0).astype(BF16).T

    basis_p = (
        left_basis.reshape(rows, n_z, n_dp, sub).transpose(0, 2, 1, 3).reshape(rows, n_dp, rows)
    )
    left_term = lax.dot_general(
        basis_p, grad_t, (((0,), (1,)), ((), ())), preferred_element_type=F32
    )
    turned = exchange(left_term.astype(BF16), DP)
    turned = jnp.sum(turned.astype(F32), axis=0).astype(BF16).reshape(n_z, sub, cols)

    turned, copies = lax.optimization_barrier(
        (exchange(turned, "z"), jnp.broadcast_to(grad_t[None], (n_dp, cols, rows)))
    )
    turned = turned.transpose(1, 0, 2).reshape(1, sub, n_z * cols)
    turned = exchange(jnp.broadcast_to(turned, (n_dp, sub, n_z * cols)), DP)

    turned, copies = lax.optimization_barrier((turned, copies))
    grad_all = exchange(copies, DP)

    basis_z = basis_z.reshape(n_z * cols, turns)
    total, send = rotate(turned.reshape(rows, n_z * cols), basis_z)
    new_first, new_second, back = update_and_back(
        core, total, swap_cores(send), moments, basis_z
    )
    back, grad_all = lax.optimization_barrier((back, grad_all))
    back = exchange(back.reshape(n_dp, sub, n_z * cols), DP)

    gram = lax.dot_general(
        grad_all, grad_t, (((1,), (0,)), ((), ())), preferred_element_type=F32
    )
    gram = (gram / D).astype(BF16).reshape(n_z, 4, half // 2, rows)
    low = lax.axis_index("z") % 2
    place = core * 2 + low
    mine = lax.dynamic_index_in_dim(gram, place, 1, keepdims=False).astype(F32)
    col = ("z", "core")
    for other, flip in ((place ^ 2, 1), (place ^ 1, 2), (place ^ 3, 3)):
        piece = lax.dynamic_index_in_dim(gram, other, 1, keepdims=False)
        pairs = [(i, i ^ flip) for i in range(2 * n_z)]
        mine = mine + lax.ppermute(piece, col, pairs).astype(F32)
    gram = mine.astype(BF16)
    back, gram = lax.optimization_barrier((back, gram))

    back = jnp.sum(back.astype(F32), axis=0).astype(BF16)
    back = back.reshape(sub, n_z, cols).transpose(1, 0, 2)
    packed = exchange(jnp.concatenate([to_tiles(back), gram], axis=1), "z")
    back = from_tiles(packed[:, : 2 * sub], cols)
    left_gram = packed[:, 2 * sub :].reshape(n_z // 2, half, rows)
    left_gram = jnp.sum(left_gram.astype(F32), axis=0)
    back = back.reshape(rows, cols).T
    back = exchange(jnp.broadcast_to(back[None], (n_dp, cols, rows)), DP)
    direction = lax.dot_general(
        basis_p, back, (((1, 2), (0, 2)), ((), ())), preferred_element_type=F32
    )
    return (left_gram.T, new_first.T, new_second.T, direction)


def solution(mesh):
    n_dp, n_col = mesh.shape["dp"], mesh.shape["col"]
    side = int(round(n_dp**0.5))
    fine = Mesh(
        mesh.devices.reshape(side, side, n_col // 2, 2), ("y", "x", "z", "core")
    )
    dp, col = ("y", "x"), ("z", "core")
    in_specs = (P(dp, None, col), P(dp, None), P(col, dp), P(dp, col), P(dp, col))
    out_specs = (P(dp, col), P(dp, col), P(dp, col), P(dp, col))
    return jax.shard_map(
        on_device, mesh=fine, in_specs=in_specs, out_specs=out_specs, check_vma=False
    )
```

```python
import jax
import jax.numpy as jnp
from jax import lax
from jax.experimental import pallas as pl
from jax.experimental.pallas import tpu as pltpu
from jax.sharding import Mesh, PartitionSpec as P

D = 7168
DP = ("y", "x")
F32 = jnp.float32
BF16 = jnp.bfloat16
LANES = 128


def exchange(chunks, axes):
    return lax.all_to_all(chunks, axes, 0, 0, tiled=True)


def swap_cores(block):
    return lax.ppermute(block, "core", [(0, 1), (1, 0)])


def to_tiles(block):
    z, sub, cols = block.shape
    block = jnp.pad(block, ((0, 0), (0, 0), (0, 2 * LANES - cols)))
    return block.reshape(z, sub, 2, LANES).transpose(0, 2, 1, 3).reshape(z, 2 * sub, LANES)


def from_tiles(block, cols):
    z, rows, _ = block.shape
    block = block.reshape(z, 2, rows // 2, LANES).transpose(0, 2, 1, 3)
    return block.reshape(z, rows // 2, 2 * LANES)[:, :, :cols]


def rotate_kernel(turned_ref, basis_ref, total_ref, send_ref):
    total = jnp.dot(turned_ref[...], basis_ref[...], preferred_element_type=F32)
    total_ref[...] = total
    send_ref[...] = total.astype(BF16)


def vmem():
    return pl.BlockSpec(memory_space=pltpu.VMEM)


def rotate(turned, basis):
    rows, depth = turned.shape
    turns = basis.shape[1]
    return pl.pallas_call(
        rotate_kernel,
        in_specs=[vmem(), vmem()],
        out_specs=[vmem(), vmem()],
        out_shape=[
            jax.ShapeDtypeStruct((rows, turns), F32),
            jax.ShapeDtypeStruct((rows, turns), BF16),
        ],
        compiler_params=pltpu.CompilerParams(vmem_limit_bytes=32 * 2**20),
        cost_estimate=pl.CostEstimate(
            flops=2 * rows * depth * turns,
            bytes_accessed=2 * depth * (rows + turns) + 6 * rows * turns,
            transcendentals=0,
        ),
    )(turned, basis)


def update_kernel(
    core_ref, total_ref, theirs_ref, moments_ref, basis_ref, first_ref, second_ref, back_ref
):
    half = first_ref.shape[0]
    updates = []
    for i in range(2):
        rows = slice(i * half, (i + 1) * half)
        rotated = total_ref[rows, :] + theirs_ref[rows, :].astype(F32)
        first = 0.9 * moments_ref[i, 0] + 0.1 * rotated
        second = 0.95 * moments_ref[i, 1] + 0.05 * rotated * rotated
        updates.append(first / 0.19 / (jnp.sqrt(second / 0.0975) + 1e-08))

        @pl.when(core_ref[0] == i)
        def _():
            first_ref[...] = first
            second_ref[...] = second

    update = jnp.concatenate(updates, axis=0).astype(BF16)
    step = 512
    for i in range(basis_ref.shape[0] // step):
        part = slice(i * step, (i + 1) * step)
        back_ref[:, part] = lax.dot_general(
            update, basis_ref[part, :], (((1,), (1,)), ((), ())), preferred_element_type=F32
        ).astype(BF16)


def update_and_back(core, total, theirs, moments, basis):
    rows, turns = total.shape
    depth = basis.shape[0]
    half = rows // 2
    return pl.pallas_call(
        update_kernel,
        in_specs=[pl.BlockSpec(memory_space=pltpu.SMEM)] + [vmem()] * 4,
        out_specs=[vmem()] * 3,
        out_shape=[
            jax.ShapeDtypeStruct((half, turns), F32),
            jax.ShapeDtypeStruct((half, turns), F32),
            jax.ShapeDtypeStruct((rows, depth), BF16),
        ],
        compiler_params=pltpu.CompilerParams(vmem_limit_bytes=32 * 2**20),
        cost_estimate=pl.CostEstimate(
            flops=2 * rows * depth * turns,
            bytes_accessed=2 * depth * (rows + turns) + 22 * rows * turns,
            transcendentals=rows * turns,
        ),
    )(core.reshape(1), total, theirs, moments, basis)


def split_kernel(source_ref, chunks_ref):
    n, _, width = chunks_ref.shape
    for i in range(n):
        chunks_ref[i] = source_ref[:, i * width : (i + 1) * width]


def split(source, n):
    rows, columns = source.shape
    return pl.pallas_call(
        split_kernel,
        in_specs=[vmem()],
        out_specs=vmem(),
        out_shape=jax.ShapeDtypeStruct((n, rows, columns // n), source.dtype),
        compiler_params=pltpu.CompilerParams(vmem_limit_bytes=32 * 2**20),
        cost_estimate=pl.CostEstimate(
            flops=0, bytes_accessed=4 * rows * columns, transcendentals=0
        ),
    )(source)


def on_device(grad_parts, left_basis, right_basis, first_moment, second_moment):
    rows = left_basis.shape[0]
    cols = right_basis.shape[0]
    turns = right_basis.shape[1]
    n_dp = left_basis.shape[1] // rows
    n_z = lax.axis_size("z")
    sub = rows // n_dp
    half = rows // 2
    core = lax.axis_index("core")

    def both(block):
        theirs = swap_cores(block)
        return jnp.where(core == 0, jnp.stack([block, theirs]), jnp.stack([theirs, block]))

    basis_z = lax.all_gather(right_basis, "z", axis=0, tiled=False)

    parts, moments = lax.optimization_barrier(
        (
            exchange(split(grad_parts[0].T, n_dp), DP),
            both(jnp.stack([first_moment.T, second_moment.T])),
        )
    )
    grad_t = jnp.sum(parts.astype(F32), axis=0).astype(BF16)

    basis_p = (
        left_basis.reshape(rows, n_z, n_dp, sub).transpose(0, 2, 1, 3).reshape(rows, n_dp, rows)
    )
    left_term = lax.dot_general(
        basis_p, grad_t, (((0,), (1,)), ((), ())), preferred_element_type=F32
    )
    turned = exchange(left_term.astype(BF16), DP)
    turned = jnp.sum(turned.astype(F32), axis=0).astype(BF16).reshape(n_z, sub, cols)

    turned, copies = lax.optimization_barrier(
        (exchange(turned, "z"), jnp.broadcast_to(grad_t[None], (n_dp, cols, rows)))
    )
    turned = turned.transpose(1, 0, 2).reshape(1, sub, n_z * cols)
    turned = exchange(jnp.broadcast_to(turned, (n_dp, sub, n_z * cols)), DP)

    turned, copies = lax.optimization_barrier((turned, copies))
    grad_all = exchange(copies, DP)

    basis_z = basis_z.reshape(n_z * cols, turns)
    total, send = rotate(turned.reshape(rows, n_z * cols), basis_z)
    new_first, new_second, back = update_and_back(
        core, total, swap_cores(send), moments, basis_z
    )
    back, grad_all = lax.optimization_barrier((back, grad_all))
    back = exchange(back.reshape(n_dp, sub, n_z * cols), DP)

    gram = lax.dot_general(
        grad_all, grad_t, (((1,), (0,)), ((), ())), preferred_element_type=F32
    )
    gram = (gram / D).astype(BF16).reshape(n_z, 4, half // 2, rows)
    low = lax.axis_index("z") % 2
    place = core * 2 + low
    mine = lax.dynamic_index_in_dim(gram, place, 1, keepdims=False).astype(F32)
    col = ("z", "core")
    for other, flip in ((place ^ 2, 1), (place ^ 1, 2), (place ^ 3, 3)):
        piece = lax.dynamic_index_in_dim(gram, other, 1, keepdims=False)
        pairs = [(i, i ^ flip) for i in range(2 * n_z)]
        mine = mine + lax.ppermute(piece, col, pairs).astype(F32)
    gram = mine.astype(BF16)
    back, gram = lax.optimization_barrier((back, gram))

    back = jnp.sum(back.astype(F32), axis=0).astype(BF16)
    back = back.reshape(sub, n_z, cols).transpose(1, 0, 2)
    packed = exchange(jnp.concatenate([to_tiles(back), gram], axis=1), "z")
    back = from_tiles(packed[:, : 2 * sub], cols)
    left_gram = packed[:, 2 * sub :].reshape(n_z // 2, half, rows)
    left_gram = jnp.sum(left_gram.astype(F32), axis=0)
    back = back.reshape(rows, cols).T
    back = exchange(jnp.broadcast_to(back[None], (n_dp, cols, rows)), DP)
    direction = lax.dot_general(
        basis_p, back, (((1, 2), (0, 2)), ((), ())), preferred_element_type=F32
    )
    return (left_gram.T, new_first.T, new_second.T, direction)


def solution(mesh):
    n_dp, n_col = mesh.shape["dp"], mesh.shape["col"]
    side = int(round(n_dp**0.5))
    fine = Mesh(
        mesh.devices.reshape(side, side, n_col // 2, 2), ("y", "x", "z", "core")
    )
    dp, col = ("y", "x"), ("z", "core")
    in_specs = (P(dp, None, col), P(dp, None), P(col, dp), P(dp, col), P(dp, col))
    out_specs = (P(dp, col), P(dp, col), P(dp, col), P(dp, col))
    return jax.shard_map(
        on_device, mesh=fine, in_specs=in_specs, out_specs=out_specs, check_vma=False
    )
```
